32 devices in a mesh: pipe: 2 (over x), row: 8 (over z, core), col: 2 (over y).
Axes of the slice: x: 2, y: 2, z: 4, core: 2. Of those that a mesh axis runs over, the one named last changes fastest.
Arguments:
- inputs: bfloat16 [4, 8, 1024, 512], P(None, 'row', 'col'), may hold values from -6 to 6
- first_gain: float32 [2, 512], P('pipe'), may hold values from 0.5 to 1.5
- first_shift: float32 [2, 512], P('pipe'), may hold values from -1.75 to 1.75
- qkv_weight: bfloat16 [2, 3, 512, 512], P('pipe', None, 'row', 'col'), may hold values from -0.25 to 0.25
- query_bias: float32 [2, 512], P('pipe', 'col'), may hold values from -3 to 3
- value_bias: float32 [2, 512], P('pipe', 'col'), may hold values from -1.75 to 1.75
- proj_weight: bfloat16 [2, 512, 512], P('pipe', 'col', 'row'), may hold values from -1 to 1
- proj_bias: float32 [2, 512], P('pipe'), may hold values from -1.75 to 1.75
- second_gain: float32 [2, 512], P('pipe'), may hold values from 0.5 to 1.5
- second_shift: float32 [2, 512], P('pipe'), may hold values from -1.75 to 1.75
- up_weight: bfloat16 [2, 512, 2048], P('pipe', 'row', 'col'), may hold values from -0.25 to 0.25
- up_bias: float32 [2, 2048], P('pipe', 'col'), may hold values from -3 to 3
- down_weight: bfloat16 [2, 2048, 512], P('pipe', 'col', 'row'), may hold values from -0.125 to 0.125
- down_bias: float32 [2, 512], P('pipe'), may hold values from -1.75 to 1.75
- cotangent: bfloat16 [4, 8, 1024, 512], P(None, 'row', 'col'), may hold values from -6 to 6
- live_clips: int32 [4, 8], P(None, 'row'), may hold values 0 or 1
Outputs:
- states: bfloat16 [2, 4, 8, 1024, 512], P('pipe', None, 'row', 'col')
- state_grads: float32 [2, 4, 8, 1024, 512], P('pipe', None, 'row', 'col')
- grad_first_gain: float32 [2, 512], P('pipe')
- grad_first_shift: float32 [2, 512], P('pipe')
- grad_qkv_weight: float32 [2, 3, 512, 512], P('pipe', None, 'row', 'col')
- grad_query_bias: float32 [2, 512], P('pipe', 'col')
- grad_value_bias: float32 [2, 512], P('pipe', 'col')
- grad_proj_weight: float32 [2, 512, 512], P('pipe', 'col', 'row')
- grad_proj_bias: float32 [2, 512], P('pipe')
- grad_second_gain: float32 [2, 512], P('pipe')
- grad_second_shift: float32 [2, 512], P('pipe')
- grad_up_weight: float32 [2, 512, 2048], P('pipe', 'row', 'col')
- grad_up_bias: float32 [2, 2048], P('pipe', 'col')
- grad_down_weight: float32 [2, 2048, 512], P('pipe', 'col', 'row')
- grad_down_bias: float32 [2, 512], P('pipe')
The draws below stay inside these ranges and needn't reach their ends.
All inputs are finite; a program needn't handle non-finite values. No bound on the sum of `live_clips` on one device may be relied on, other than what follows from the above.
Results may differ from the reference program's by a relative error of at most 0.015.
Values may be sent and summed in bfloat16 or wider, within the bound.
A program may use at most 192 MiB of HBM per device.

```python
import math
import jax
import jax.numpy as jnp
from jax import lax

D = 512
HD = 64
FF = 2048
SEQ = 1024
LAYERS = 2
MICRO = 4
CLIPS = 8


def set_ends(array, rng, least, high):
    longest = array.shape.index(max(array.shape))
    spots = []
    for shift in (0, 1):
        where = [jax.random.randint(jax.random.fold_in(rng, axis), (), 0, length) for axis, length in enumerate(array.shape)]
        where[longest] = (where[longest] + shift) % array.shape[longest]
        spots.append(tuple(where))
    return array.at[spots[0]].set(least).at[spots[1]].set(high)


def levels(own_key, dims, cuts, least, top_value):
    def one(dim, blocks):
        steps = jax.random.uniform(jax.random.fold_in(jax.random.fold_in(own_key, 6), dim), (blocks,), jnp.float32, least / len(cuts), top_value / len(cuts))
        return jnp.repeat(jnp.exp(steps), dims[dim] // blocks).reshape((-1,) + (1,) * (len(dims) - dim - 1))

    level = one(*cuts[0])
    for cut in cuts[1:]:
        level = level * one(*cut)
    return level


def noise(own_key, extent, width, reach, pieces=(), dtype=jnp.bfloat16):
    drawn = jax.random.normal(own_key, extent, jnp.float32) * width
    if len(pieces) > 0:
        drawn = levels(own_key, extent, pieces, -0.22, 0.18) * drawn
    return jnp.clip(drawn, min=-reach, max=reach).astype(dtype)


def setup_inputs(seed: int = 0) -> dict:
    arg_keys = jax.random.split(jax.random.key(seed), 17)
    return {
        "inputs": noise(arg_keys[0], (MICRO, CLIPS, SEQ, D), 1.0, 6.0, ((1, 8), (2, 2))),
        "first_gain": jnp.clip(1.0 + 0.1 * jax.random.normal(arg_keys[1], (LAYERS, D), jnp.float32), 0.5, 1.5),
        "first_shift": noise(arg_keys[2], (LAYERS, D), 0.3, 1.75, ((0, 2),), jnp.float32),
        "qkv_weight": noise(arg_keys[3], (LAYERS, 3, D, D), D ** -0.5, 0.25, ((0, 2), (2, 8), (3, 2))),
        "query_bias": noise(arg_keys[4], (LAYERS, D), 0.5, 3.0, ((0, 2), (1, 2)), jnp.float32),
        "value_bias": noise(arg_keys[5], (LAYERS, D), 0.3, 1.75, ((0, 2), (1, 2)), jnp.float32),
        "proj_weight": noise(arg_keys[6], (LAYERS, D, D), (D // 16) ** -0.5, 1.0, ((0, 2), (1, 2), (2, 8))),
        "proj_bias": noise(arg_keys[7], (LAYERS, D), 0.3, 1.75, ((0, 2),), jnp.float32),
        "second_gain": jnp.clip(1.0 + 0.1 * jax.random.normal(arg_keys[8], (LAYERS, D), jnp.float32), 0.5, 1.5),
        "second_shift": noise(arg_keys[9], (LAYERS, D), 0.3, 1.75, ((0, 2),), jnp.float32),
        "up_weight": noise(arg_keys[10], (LAYERS, D, FF), D ** -0.5, 0.25, ((0, 2), (1, 8), (2, 2))),
        "up_bias": noise(arg_keys[11], (LAYERS, FF), 0.5, 3.0, ((0, 2), (1, 2)), jnp.float32),
        "down_weight": noise(arg_keys[12], (LAYERS, FF, D), FF ** -0.5, 0.125, ((0, 2), (1, 2), (2, 8))),
        "down_bias": noise(arg_keys[13], (LAYERS, D), 0.3, 1.75, ((0, 2),), jnp.float32),
        "cotangent": noise(arg_keys[14], (MICRO, CLIPS, SEQ, D), 1.0, 6.0, ((1, 8), (2, 2))),
        "live_clips": set_ends((jax.random.randint(arg_keys[15], (MICRO, CLIPS), 0, 5) < 4).astype(jnp.int32), jax.random.fold_in(arg_keys[15], 1), 0, 1),
    }


@jax.custom_vjp
def low(v):
    return lax.optimization_barrier(v.astype(jnp.bfloat16)).astype(jnp.float32)

@jax.custom_vjp
def low_back(v):
    return v

def low_keep(v):
    return (low(v), None)

def low_pass(kept, grad):
    return (grad,)

def back_keep(v):
    return (v, None)

def back_low(kept, grad):
    return (low(grad),)
low.defvjp(low_keep, low_pass)
low_back.defvjp(back_keep, back_low)
epsilon = 1e-05

def layer_norm(values, gain, shift):
    row_mean = lax.optimization_barrier(jnp.mean(values, axis=-1, keepdims=True))
    row_var = lax.optimization_barrier(jnp.mean(jnp.square(values - row_mean), axis=-1, keepdims=True))
    return (values - row_mean) * lax.rsqrt(row_var + epsilon) * gain + shift

def encoder_layer(layer_params, values):
    first_gain, first_shift, qkv_weight, query_bias, value_bias, proj_weight, proj_bias, second_gain, second_shift, up_weight, up_bias, down_weight, down_bias = layer_params
    highest = lax.Precision.HIGHEST
    head_count = D // HD
    normed_one = low(layer_norm(values, first_gain, first_shift))
    query_heads = low(low_back(jnp.dot(normed_one, qkv_weight[0], precision=highest)) + query_bias).reshape(SEQ, head_count, HD)
    key_heads = low(low_back(jnp.dot(normed_one, qkv_weight[1], precision=highest))).reshape(SEQ, head_count, HD)
    value_heads = low(low_back(jnp.dot(normed_one, qkv_weight[2], precision=highest)) + value_bias).reshape(SEQ, head_count, HD)
    scores = low_back(jnp.einsum('qhd,khd->hqk', query_heads, key_heads, precision=highest) * (1.0 / math.sqrt(HD)))
    softmax_out = low(jax.nn.softmax(scores, axis=-1))
    context = low(low_back(jnp.einsum('hqk,khd->qhd', softmax_out, value_heads, precision=highest).reshape(SEQ, D)))
    hidden = values + low_back(jnp.dot(context, proj_weight, precision=highest)) + proj_bias
    normed_two = low(layer_norm(hidden, second_gain, second_shift))
    pre_act = low_back(jnp.dot(normed_two, up_weight, precision=highest)) + up_bias
    activated = low(jax.nn.gelu(pre_act, approximate=False))
    return hidden + low_back(jnp.dot(activated, down_weight, precision=highest)) + down_bias

def clip_layers(params, clip_rows, offset):
    first = encoder_layer(tuple((part[0] for part in params)), clip_rows)
    sent = low(low_back(first)) + offset
    return (sent, encoder_layer(tuple((part[1] for part in params)), sent))

def reference(inputs, first_gain, first_shift, qkv_weight, query_bias, value_bias, proj_weight, proj_bias, second_gain, second_shift, up_weight, up_bias, down_weight, down_bias, cotangent, live_clips):
    params = tuple((part.astype(jnp.float32) for part in (first_gain, first_shift, qkv_weight, query_bias, value_bias, proj_weight, proj_bias, second_gain, second_shift, up_weight, up_bias, down_weight, down_bias)))
    clip_count = MICRO * CLIPS
    clips = inputs.reshape(clip_count, SEQ, D).astype(jnp.float32)
    offsets = jnp.zeros_like(clips)

    def forward(clips, offsets, params):

        def per_clip(pair):
            return clip_layers(params, pair[0], pair[1])
        return lax.map(jax.checkpoint(per_clip), (clips, offsets))
    (sent, final), pull = jax.vjp(forward, clips, offsets, params)
    live_weight = live_clips.reshape(clip_count).astype(jnp.float32)
    cot_rows = cotangent.reshape(clip_count, SEQ, D).astype(jnp.float32) * live_weight[:, None, None]
    grad_clips, grad_offsets, grad_params = pull((jnp.zeros_like(sent), cot_rows))
    states = jnp.stack([sent, final]).reshape(LAYERS, MICRO, CLIPS, SEQ, D).astype(jnp.bfloat16)
    state_grads = jnp.stack([grad_clips, grad_offsets]).reshape(LAYERS, MICRO, CLIPS, SEQ, D)
    return (states, state_grads, grad_params[0], grad_params[1], grad_params[2], grad_params[3], grad_params[4], grad_params[5], grad_params[6], grad_params[7], grad_params[8], grad_params[9], grad_params[10], grad_params[11], grad_params[12])
```

```python
import math

import jax
import jax.numpy as jnp
from jax import lax
from jax.experimental import pallas as pl
from jax.experimental.pallas import tpu as pltpu
from jax.sharding import PartitionSpec as P

HD = 64


epsilon = 1e-05


def from_behind(value, axis, steps):
    count = lax.axis_size(axis)
    first, last = (max(0, -steps), min(count, count - steps))
    return lax.ppermute(value, axis, [(source, source + steps) for source in range(first, last)])


def exact_gelu(values):
    return jax.nn.gelu(values, approximate=False)


def spread_features(normed):
    return lax.all_gather(normed, "col", axis=0, tiled=True)


def sum_columns(partial_rows):
    return lax.psum_scatter(partial_rows, "col", scatter_dimension=0, tiled=True)


def spread_grads(grad_low):
    return lax.all_gather(grad_low, "col", axis=0, tiled=True)


def sum_grad_columns(partial_rows):
    return lax.psum_scatter(partial_rows, "col", scatter_dimension=0, tiled=True)


def norm_forward(values, gain, shift):
    row_mean = jnp.mean(values, axis=-1, keepdims=True)
    row_var = jnp.mean(jnp.square(values - row_mean), axis=-1, keepdims=True)
    inv_std = lax.rsqrt(row_var + epsilon)
    centered = (values - row_mean) * inv_std
    return (centered, inv_std[:, 0], (centered * gain + shift).astype(jnp.bfloat16))


def norm_backward(grad_norm, centered, inv_std, gain):
    grad_gain = jnp.sum(grad_norm * centered, axis=0)
    grad_shift = jnp.sum(grad_norm, axis=0)
    scaled = grad_norm * gain
    first = jnp.mean(scaled, axis=-1, keepdims=True)
    second = jnp.mean(scaled * centered, axis=-1, keepdims=True)
    grad_in = inv_std[:, None] * (scaled - first - centered * second)
    return (grad_in, grad_gain, grad_shift)


def attention_probs(query_heads, key_heads):
    score_scale = 1.0 / math.sqrt(HD)
    scores = (
        jnp.einsum("qhd,khd->hqk", query_heads, key_heads, preferred_element_type=jnp.float32)
        * score_scale
    )
    return jax.nn.softmax(scores, axis=-1)


def layer_forward(values, weights, params):
    qkv_full, proj_full, up_full, down_full = weights
    (
        gain_one,
        shift_one,
        query_bias,
        value_bias,
        proj_bias,
        gain_two,
        shift_two,
        up_bias,
        down_bias,
    ) = params
    head_count = qkv_full.shape[2] // HD
    centered_one, inv_one, normed_one = norm_forward(values, gain_one, shift_one)
    attn_input = spread_features(normed_one)
    frame_count = attn_input.shape[0]
    projected = jnp.einsum("sd,jde->jse", attn_input, qkv_full, preferred_element_type=jnp.float32)
    query_heads = (
        (projected[0] + query_bias).astype(jnp.bfloat16).reshape(frame_count, head_count, HD)
    )
    key_heads = projected[1].astype(jnp.bfloat16).reshape(frame_count, head_count, HD)
    value_heads = (
        (projected[2] + value_bias).astype(jnp.bfloat16).reshape(frame_count, head_count, HD)
    )
    softmax_out = attention_probs(query_heads, key_heads)
    context = jnp.einsum(
        "hqk,khd->qhd",
        softmax_out.astype(jnp.bfloat16),
        value_heads,
        preferred_element_type=jnp.float32,
    )
    context = context.reshape(frame_count, head_count * HD).astype(jnp.bfloat16)
    attended = (
        sum_columns(jnp.dot(context, proj_full, preferred_element_type=jnp.float32)) + proj_bias
    )
    hidden = values + attended
    centered_two, inv_two, normed_two = norm_forward(hidden, gain_two, shift_two)
    mlp_input = spread_features(normed_two)
    pre_act = jnp.dot(mlp_input, up_full, preferred_element_type=jnp.float32) + up_bias
    activated = exact_gelu(pre_act).astype(jnp.bfloat16)
    output = (
        hidden
        + sum_columns(jnp.dot(activated, down_full, preferred_element_type=jnp.float32))
        + down_bias
    )
    kept = (
        centered_one,
        inv_one,
        attn_input,
        query_heads,
        key_heads,
        value_heads,
        context,
        centered_two,
        inv_two,
        mlp_input,
        pre_act,
        activated,
    )
    return (output, kept)


def layer_backward(grad_out, kept, weights, params):
    qkv_full, proj_full, up_full, down_full = weights
    (
        gain_one,
        shift_one,
        query_bias,
        value_bias,
        proj_bias,
        gain_two,
        shift_two,
        up_bias,
        down_bias,
    ) = params
    (
        centered_one,
        inv_one,
        attn_input,
        query_heads,
        key_heads,
        value_heads,
        context,
        centered_two,
        inv_two,
        mlp_input,
        pre_act,
        activated,
    ) = kept
    frame_count = attn_input.shape[0]
    score_scale = 1.0 / math.sqrt(HD)
    grad_down_bias = jnp.sum(grad_out, axis=0)
    down_grad = spread_grads(grad_out.astype(jnp.bfloat16))
    grad_down = jnp.einsum("sf,sd->fd", activated, down_grad, preferred_element_type=jnp.float32)
    grad_act = jnp.einsum("sd,fd->sf", down_grad, down_full, preferred_element_type=jnp.float32)
    unused, gelu_pull = jax.vjp(exact_gelu, pre_act)
    grad_pre = gelu_pull(grad_act)[0]
    grad_up_bias = jnp.sum(grad_pre, axis=0)
    grad_pre_low = grad_pre.astype(jnp.bfloat16)
    grad_up = jnp.einsum("sd,sf->df", mlp_input, grad_pre_low, preferred_element_type=jnp.float32)
    grad_normed_two = sum_grad_columns(
        jnp.einsum("sf,df->sd", grad_pre_low, up_full, preferred_element_type=jnp.float32)
    )
    grad_hidden_norm, grad_gain_two, grad_shift_two = norm_backward(
        grad_normed_two, centered_two, inv_two, gain_two
    )
    grad_hidden = grad_out + grad_hidden_norm
    grad_proj_bias = jnp.sum(grad_hidden, axis=0)
    proj_grad = spread_grads(grad_hidden.astype(jnp.bfloat16))
    grad_proj = jnp.einsum("se,sd->ed", context, proj_grad, preferred_element_type=jnp.float32)
    grad_context = jnp.einsum("sd,ed->se", proj_grad, proj_full, preferred_element_type=jnp.float32)
    grad_context = grad_context.astype(jnp.bfloat16).reshape(query_heads.shape)
    softmax_out = attention_probs(query_heads, key_heads)
    grad_probs = jnp.einsum(
        "qhd,khd->hqk", grad_context, value_heads, preferred_element_type=jnp.float32
    )
    grad_value = jnp.einsum(
        "hqk,qhd->khd",
        softmax_out.astype(jnp.bfloat16),
        grad_context,
        preferred_element_type=jnp.float32,
    )
    grad_scores = softmax_out * (
        grad_probs - jnp.sum(softmax_out * grad_probs, axis=-1, keepdims=True)
    )
    scores_low = grad_scores.astype(jnp.bfloat16)
    grad_query = (
        jnp.einsum("hqk,khd->qhd", scores_low, key_heads, preferred_element_type=jnp.float32)
        * score_scale
    )
    grad_key = (
        jnp.einsum("hqk,qhd->khd", scores_low, query_heads, preferred_element_type=jnp.float32)
        * score_scale
    )
    grad_query = grad_query.reshape(frame_count, -1)
    grad_key = grad_key.reshape(frame_count, -1)
    grad_value = grad_value.reshape(frame_count, -1)
    grad_query_bias = jnp.sum(grad_query, axis=0)
    grad_value_bias = jnp.sum(grad_value, axis=0)
    grad_qkv_low = jnp.stack([grad_query, grad_key, grad_value]).astype(jnp.bfloat16)
    grad_qkv = jnp.einsum(
        "sd,jse->jde", attn_input, grad_qkv_low, preferred_element_type=jnp.float32
    )
    grad_normed_one = sum_grad_columns(
        jnp.einsum("jse,jde->sd", grad_qkv_low, qkv_full, preferred_element_type=jnp.float32)
    )
    grad_in_norm, grad_gain_one, grad_shift_one = norm_backward(
        grad_normed_one, centered_one, inv_one, gain_one
    )
    grad_in = grad_hidden + grad_in_norm
    weight_grads = (grad_qkv, grad_proj, grad_up, grad_down)
    vector_grads = (
        grad_gain_one,
        grad_shift_one,
        grad_query_bias,
        grad_value_bias,
        grad_proj_bias,
        grad_gain_two,
        grad_shift_two,
        grad_up_bias,
        grad_down_bias,
    )
    return (grad_in, weight_grads, vector_grads)


def store_slot(buffer, slot_index, is_valid, value):
    current = lax.dynamic_index_in_dim(buffer, slot_index, 0, keepdims=False)
    return lax.dynamic_update_index_in_dim(
        buffer, jnp.where(is_valid, value, current), slot_index, 0
    )


def reduce_end(weight_acc):
    return (
        lax.psum_scatter(
            weight_acc[0].astype(jnp.bfloat16), "row", scatter_dimension=1, tiled=True
        ).astype(jnp.float32),
        lax.psum_scatter(
            weight_acc[1].astype(jnp.bfloat16), "row", scatter_dimension=1, tiled=True
        ).astype(jnp.float32),
        lax.psum_scatter(
            weight_acc[2].astype(jnp.bfloat16), "row", scatter_dimension=0, tiled=True
        ).astype(jnp.float32),
        lax.psum_scatter(
            weight_acc[3].astype(jnp.bfloat16), "row", scatter_dimension=1, tiled=True
        ).astype(jnp.float32),
    )


def on_device(
    inputs,
    first_gain,
    first_shift,
    qkv_weight,
    query_bias,
    value_bias,
    proj_weight,
    proj_bias,
    second_gain,
    second_shift,
    up_weight,
    up_bias,
    down_weight,
    down_bias,
    cotangent,
    live_clips,
):
    micro_count = inputs.shape[0]
    row_count = inputs.shape[2]
    feature_count = inputs.shape[3]
    section_index = lax.axis_index("pipe")
    weights = (
        lax.all_gather(qkv_weight[0], "row", axis=1, tiled=True),
        lax.all_gather(proj_weight[0], "row", axis=1, tiled=True),
        lax.all_gather(up_weight[0], "row", axis=0, tiled=True),
        lax.all_gather(down_weight[0], "row", axis=1, tiled=True),
    )
    params = (
        first_gain[0],
        first_shift[0],
        query_bias[0],
        value_bias[0],
        proj_bias[0],
        second_gain[0],
        second_shift[0],
        up_bias[0],
        down_bias[0],
    )
    kept_buffers = ()
    zero_rows = jnp.zeros((row_count, feature_count), jnp.bfloat16)
    zero_stack = jnp.zeros((micro_count, row_count, feature_count), jnp.bfloat16)
    own_inputs = inputs[:, 0]

    def forward_tick(state_carry, tick_index):
        received, outputs, layer_inputs, buffers = state_carry
        batch_index = tick_index - section_index
        is_valid = (batch_index >= 0) & (batch_index < micro_count)
        slot_index = jnp.clip(batch_index, 0, micro_count - 1)
        own_input = lax.dynamic_index_in_dim(
            own_inputs, jnp.minimum(tick_index, micro_count - 1), 0, keepdims=False
        )
        layer_input = jnp.where(section_index == 0, own_input, received)
        output, kept = layer_forward(layer_input.astype(jnp.float32), weights, params)
        output_low = output.astype(jnp.bfloat16)
        passed = from_behind(output_low, "pipe", 1)
        outputs = store_slot(outputs, slot_index, is_valid, output_low)
        layer_inputs = store_slot(layer_inputs, slot_index, is_valid, layer_input)
        return ((passed, outputs, layer_inputs, buffers), None)

    tick_range = jnp.arange(micro_count + 1)
    forward_out, unused = lax.scan(
        forward_tick, (zero_rows, zero_stack, zero_stack, kept_buffers), tick_range
    )
    unused_rows, outputs, layer_inputs, kept_buffers = forward_out
    weight_acc = tuple((jnp.zeros(part.shape, jnp.float32) for part in weights))
    vector_acc = tuple((jnp.zeros(part.shape, jnp.float32) for part in params))
    grads_init = jnp.zeros((micro_count, row_count, feature_count), jnp.float32)
    live_rows = live_clips[:, 0]
    cot_rows_all = cotangent[:, 0]

    def backward_tick(state_carry, tick_index):
        received, grads_in, weight_sum, vector_sum = state_carry
        batch_index = micro_count - tick_index - section_index
        is_valid = (batch_index >= 0) & (batch_index < micro_count)
        slot_index = jnp.clip(batch_index, 0, micro_count - 1)
        cot_rows = lax.dynamic_index_in_dim(cot_rows_all, slot_index, 0, keepdims=False).astype(
            jnp.float32
        )
        live_flag = lax.dynamic_index_in_dim(live_rows, slot_index, 0, keepdims=False).astype(
            jnp.float32
        )
        grad_out = jnp.where(
            section_index == 1, cot_rows * live_flag, received.astype(jnp.float32)
        ) * is_valid.astype(jnp.float32)
        stored_input = lax.dynamic_index_in_dim(layer_inputs, slot_index, 0, keepdims=False)
        kept = layer_forward(stored_input.astype(jnp.float32), weights, params)[1]
        grad_in, weight_grads, vector_grads = layer_backward(grad_out, kept, weights, params)
        passed = from_behind(grad_in.astype(jnp.bfloat16), "pipe", -1)
        grads_in = store_slot(grads_in, slot_index, is_valid, grad_in)
        weight_sum = jax.tree.map(jnp.add, weight_sum, weight_grads)
        vector_sum = jax.tree.map(jnp.add, vector_sum, vector_grads)
        return ((passed, grads_in, weight_sum, vector_sum), None)

    backward_out, unused_two = lax.scan(
        backward_tick, (zero_rows, grads_init, weight_acc, vector_acc), tick_range
    )
    unused_grad, grads_in, weight_acc, vector_acc = backward_out
    weight_out = reduce_end(weight_acc)
    split_out = lax.psum((vector_acc[2], vector_acc[3], vector_acc[7]), "row")
    whole_out = lax.psum(
        (vector_acc[0], vector_acc[1], vector_acc[4], vector_acc[5], vector_acc[6], vector_acc[8]),
        ("row", "col"),
    )
    return (
        outputs[None, :, None],
        grads_in[None, :, None],
        whole_out[0][None],
        whole_out[1][None],
        weight_out[0][None],
        split_out[0][None],
        split_out[1][None],
        weight_out[1][None],
        whole_out[2][None],
        whole_out[3][None],
        whole_out[4][None],
        weight_out[2][None],
        split_out[2][None],
        weight_out[3][None],
        whole_out[5][None],
    )


def contract(left, right, left_dim, right_dim):
    return lax.dot_general(
        left, right, (((left_dim,), (right_dim,)), ((), ())), preferred_element_type=jnp.float32
    )


QUERY_BLOCK = 256


def attention_forward_kernel(q_ref, k_ref, v_ref, context_ref, lse_ref):
    frames = q_ref.shape[0]
    score_scale = 1.0 / math.sqrt(HD)
    for start in range(0, frames, QUERY_BLOCK):
        rows = slice(start, start + QUERY_BLOCK)
        parts = []
        for head in range(2):
            lanes = slice(head * HD, (head + 1) * HD)
            scaled = q_ref[rows, lanes] * jnp.asarray(score_scale, jnp.bfloat16)
            scores = contract(k_ref[:, lanes], scaled, 1, 1)
            top = jnp.max(scores, axis=0, keepdims=True)
            weights = jnp.exp(scores - top)
            total = jnp.sum(weights, axis=0, keepdims=True)
            mixed = contract(v_ref[:, lanes], weights.astype(jnp.bfloat16), 0, 0)
            parts.append(mixed / total)
            lse_ref[0, head : head + 1, rows] = top + jnp.log(total)
        pair = jnp.concatenate(parts, axis=0)
        context_ref[rows, :] = pair.T.astype(jnp.bfloat16)


def attention_forward(qkv):
    frames = qkv.shape[0]
    width = qkv.shape[1] // 3
    pairs = width // (2 * HD)

    def column(part):
        return pl.BlockSpec((frames, 2 * HD), lambda pair: (0, pair + part * pairs))

    return pl.pallas_call(
        attention_forward_kernel,
        grid=(pairs,),
        in_specs=[column(0), column(1), column(2)],
        out_specs=[
            pl.BlockSpec((frames, 2 * HD), lambda pair: (0, pair)),
            pl.BlockSpec((1, 8, frames), lambda pair: (pair, 0, 0)),
        ],
        out_shape=[
            jax.ShapeDtypeStruct((frames, width), jnp.bfloat16),
            jax.ShapeDtypeStruct((pairs, 8, frames), jnp.float32),
        ],
        compiler_params=pltpu.CompilerParams(vmem_limit_bytes=40 * 1024 * 1024),
        cost_estimate=pl.CostEstimate(
            flops=4 * frames * frames * width,
            bytes_accessed=8 * frames * width,
            transcendentals=frames * frames * width // HD,
        ),
        name="attention_forward",
    )(qkv, qkv, qkv)


def attention_backward_kernel(q_ref, k_ref, v_ref, grad_ref, lse_ref, out_ref, bias_ref):
    frames = q_ref.shape[0]
    width = out_ref.shape[1] // 3
    pair_index = pl.program_id(0)
    score_scale = 1.0 / math.sqrt(HD)
    grad_keys = [None, None]
    grad_values = [None, None]
    query_total = jnp.zeros((1, 2 * HD), jnp.float32)

    def columns(part):
        return pl.ds(pl.multiple_of(part * width + pair_index * (2 * HD), 2 * HD), 2 * HD)

    for start in range(0, frames, QUERY_BLOCK):
        rows = slice(start, start + QUERY_BLOCK)
        parts = []
        for head in range(2):
            lanes = slice(head * HD, (head + 1) * HD)
            keys = k_ref[:, lanes]
            grads = grad_ref[rows, lanes]
            scaled = q_ref[rows, lanes] * jnp.asarray(score_scale, jnp.bfloat16)
            scores = contract(keys, scaled, 1, 1)
            probs = jnp.exp(scores - lse_ref[0, head : head + 1, rows])
            grad_probs = contract(v_ref[:, lanes], grads, 1, 1)
            delta = jnp.sum(probs * grad_probs, axis=0, keepdims=True)
            low_scores = (probs * (grad_probs - delta)).astype(jnp.bfloat16)
            value_part = contract(probs.astype(jnp.bfloat16), grads, 1, 0)
            key_part = contract(low_scores, scaled, 1, 0)
            grad_values[head] = value_part if start == 0 else grad_values[head] + value_part
            grad_keys[head] = key_part if start == 0 else grad_keys[head] + key_part
            parts.append(contract(keys, low_scores, 0, 0))
        pair = jnp.concatenate(parts, axis=0).T * score_scale
        query_total = query_total + jnp.sum(pair, axis=0, keepdims=True)
        out_ref[rows, columns(0)] = pair.astype(jnp.bfloat16)
    key_pair = jnp.concatenate(grad_keys, axis=1)
    value_pair = jnp.concatenate(grad_values, axis=1)
    out_ref[:, columns(1)] = key_pair.astype(jnp.bfloat16)
    out_ref[:, columns(2)] = value_pair.astype(jnp.bfloat16)
    bias_ref[0:1, columns(0)] = query_total
    bias_ref[0:1, columns(2)] = jnp.sum(value_pair, axis=0, keepdims=True)


def attention_backward(qkv, grad_context, lse):
    frames = qkv.shape[0]
    width = qkv.shape[1] // 3
    pairs = width // (2 * HD)

    def column(part):
        return pl.BlockSpec((frames, 2 * HD), lambda pair: (0, pair + part * pairs))

    return pl.pallas_call(
        attention_backward_kernel,
        grid=(pairs,),
        in_specs=[
            column(0),
            column(1),
            column(2),
            column(0),
            pl.BlockSpec((1, 8, frames), lambda pair: (pair, 0, 0)),
        ],
        out_specs=[
            pl.BlockSpec((frames, 3 * width), lambda pair: (0, 0)),
            pl.BlockSpec((8, 3 * width), lambda pair: (0, 0)),
        ],
        out_shape=[
            jax.ShapeDtypeStruct((frames, 3 * width), jnp.bfloat16),
            jax.ShapeDtypeStruct((8, 3 * width), jnp.float32),
        ],
        compiler_params=pltpu.CompilerParams(vmem_limit_bytes=40 * 1024 * 1024),
        cost_estimate=pl.CostEstimate(
            flops=10 * frames * frames * width,
            bytes_accessed=14 * frames * width,
            transcendentals=frames * frames * width // HD,
        ),
        name="attention_backward",
    )(qkv, qkv, qkv, grad_context, lse)


def cut_block(block, width, hidden):
    edge = 4 * width
    return (
        block[:, : 3 * width],
        block[:, 3 * width : edge],
        block[:, edge : edge + hidden],
        block[:, edge + hidden :],
    )


def clip_forward(values, blocks, params):
    (
        gain_one,
        shift_one,
        qkv_bias,
        proj_bias,
        gain_two,
        shift_two,
        up_bias,
        down_bias,
    ) = params
    centered_one, inv_one, normed_one = norm_forward(values, gain_one, shift_one)
    qkv_parts, contexts, lses, pre_acts, activated = [], [], [], [], []
    attended = proj_bias
    for (qkv_full, proj_turned, up_full, down_turned), bias in zip(blocks, qkv_bias):
        qkv = (contract(normed_one, qkv_full, 1, 0) + bias).astype(jnp.bfloat16)
        context, lse = attention_forward(qkv)
        attended = attended + contract(context, proj_turned, 1, 1)
        qkv_parts.append(qkv)
        contexts.append(context)
        lses.append(lse)
    hidden = values + attended
    centered_two, inv_two, normed_two = norm_forward(hidden, gain_two, shift_two)
    output = hidden + down_bias
    for (qkv_full, proj_turned, up_full, down_turned), bias in zip(blocks, up_bias):
        pre_act = contract(normed_two, up_full, 1, 0) + bias
        active = exact_gelu(pre_act).astype(jnp.bfloat16)
        output = output + contract(active, down_turned, 1, 1)
        pre_acts.append(pre_act)
        activated.append(active)
    kept = (
        centered_one,
        inv_one,
        normed_one,
        qkv_parts,
        contexts,
        lses,
        centered_two,
        inv_two,
        normed_two,
        pre_acts,
        activated,
    )
    return (output, kept)


def clip_backward(grad_out, kept, blocks, params):
    gain_one, gain_two = (params[0], params[4])
    (
        centered_one,
        inv_one,
        normed_one,
        qkv_parts,
        contexts,
        lses,
        centered_two,
        inv_two,
        normed_two,
        pre_acts,
        activated,
    ) = kept
    grad_down_bias = jnp.sum(grad_out, axis=0)
    down_grad = grad_out.astype(jnp.bfloat16)
    grad_normed_two = 0.0
    up_biases, early, late, query_biases, value_biases = [], [], [], [], []
    for (qkv_full, proj_turned, up_full, down_turned), pre_act, active in zip(
        blocks, pre_acts, activated
    ):
        grad_down = contract(down_grad, active, 0, 0)
        grad_act = contract(down_grad, down_turned, 1, 0)
        grad_pre = jax.vjp(exact_gelu, pre_act)[1](grad_act)[0]
        up_biases.append(jnp.sum(grad_pre, axis=0))
        grad_pre_low = grad_pre.astype(jnp.bfloat16)
        grad_up = contract(normed_two, grad_pre_low, 0, 0)
        grad_normed_two = grad_normed_two + contract(grad_pre_low, up_full, 1, 1)
        early.append((grad_up.astype(jnp.bfloat16), grad_down.astype(jnp.bfloat16)))
    grad_hidden_norm, grad_gain_two, grad_shift_two = norm_backward(
        grad_normed_two, centered_two, inv_two, gain_two
    )
    grad_hidden = grad_out + grad_hidden_norm
    grad_proj_bias = jnp.sum(grad_hidden, axis=0)
    proj_grad = grad_hidden.astype(jnp.bfloat16)
    grad_normed_one = 0.0
    for (qkv_full, proj_turned, up_full, down_turned), qkv, context, lse in zip(
        blocks, qkv_parts, contexts, lses
    ):
        width = context.shape[1]
        grad_proj = contract(proj_grad, context, 0, 0)
        grad_context = contract(proj_grad, proj_turned, 1, 0).astype(jnp.bfloat16)
        grad_qkv_low, bias_rows = attention_backward(qkv, grad_context, lse)
        query_biases.append(bias_rows[0, :width])
        value_biases.append(bias_rows[0, 2 * width :])
        grad_qkv = contract(normed_one, grad_qkv_low, 0, 0)
        grad_normed_one = grad_normed_one + contract(grad_qkv_low, qkv_full, 1, 1)
        late.append((grad_qkv.astype(jnp.bfloat16), grad_proj.astype(jnp.bfloat16)))
    grad_in_norm, grad_gain_one, grad_shift_one = norm_backward(
        grad_normed_one, centered_one, inv_one, gain_one
    )
    grad_in = grad_hidden + grad_in_norm
    whole = jnp.concatenate(
        [
            grad_gain_one,
            grad_shift_one,
            grad_proj_bias,
            grad_gain_two,
            grad_shift_two,
            grad_down_bias,
        ]
    )
    split = jnp.stack(
        [jnp.concatenate(part) for part in zip(query_biases, value_biases, up_biases)]
    )
    return (grad_in, early, late, whole, split)


GROUP = ("pipe", "col")
EVERY = ("pipe", "col", "row")


def trade(pieces, place, targets):
    count = len(pieces)
    stacked = jnp.stack(pieces)
    taken = [lax.dynamic_index_in_dim(stacked, place, 0, keepdims=False)]
    for step in range(1, count):
        sent = lax.dynamic_index_in_dim(stacked, place ^ step, 0, keepdims=False)
        taken.append(
            lax.ppermute(
                sent,
                GROUP,
                [(here, here ^ step) for here in range(count) if here ^ step in targets],
            )
        )
    return taken


def in_order(taken, place):
    stacked = jnp.stack(taken)
    return jnp.stack(
        [
            lax.dynamic_index_in_dim(stacked, place ^ index, 0, keepdims=False)
            for index in range(len(taken))
        ]
    )


def swap_columns(own, other, col):
    got = lax.ppermute(other, "col", [(0, 1), (1, 0)])
    return jnp.where(
        col == 0, jnp.concatenate([own, got]), jnp.concatenate([got, own])
    )


def gather_blocks(block):
    full = lax.all_gather(block, EVERY, axis=0, tiled=True)
    return full.reshape(lax.axis_size(GROUP), -1, block.shape[1])


def on_device_clip(
    inputs,
    first_gain,
    first_shift,
    qkv_weight,
    query_bias,
    value_bias,
    proj_weight,
    proj_bias,
    second_gain,
    second_shift,
    up_weight,
    up_bias,
    down_weight,
    down_bias,
    cotangent,
    live_clips,
):
    section, col = (lax.axis_index("pipe"), lax.axis_index("col"))
    place = 2 * section + col
    width, hidden_width = (qkv_weight.shape[3], up_weight.shape[2])
    features = inputs.shape[3]
    half = inputs.shape[2]
    early_block = jnp.concatenate(
        [qkv_weight[0, 0], qkv_weight[0, 1], qkv_weight[0, 2], proj_weight[0].T], axis=1
    )
    late_block = jnp.concatenate([up_weight[0], down_weight[0].T], axis=1)
    early_full = gather_blocks(early_block)
    late_full = gather_blocks(late_block)
    vectors = lax.all_gather(
        jnp.concatenate(
            [
                first_gain[0],
                first_shift[0],
                proj_bias[0],
                second_gain[0],
                second_shift[0],
                down_bias[0],
                query_bias[0],
                value_bias[0],
                up_bias[0],
            ]
        ),
        GROUP,
        axis=0,
        tiled=False,
    )
    blocks, params = ([], [])
    for layer in range(2):
        blocks.append(
            [
                (
                    early_full[2 * layer + part][:, : 3 * width],
                    early_full[2 * layer + part][:, 3 * width :],
                    late_full[2 * layer + part][:, :hidden_width],
                    late_full[2 * layer + part][:, hidden_width:],
                )
                for part in range(2)
            ]
        )
        rows = vectors[2 * layer]
        whole = [rows[index * features : (index + 1) * features] for index in range(6)]
        tails = [vectors[2 * layer + part][6 * features :] for part in range(2)]
        params.append(
            (
                whole[0],
                whole[1],
                [
                    jnp.concatenate(
                        [tail[:width], jnp.zeros((width,), jnp.float32), tail[width : 2 * width]]
                    )
                    for tail in tails
                ],
                whole[2],
                whole[3],
                whole[4],
                [tail[2 * width :] for tail in tails],
                whole[5],
            )
        )

    def own_clip(rows):
        own = lax.dynamic_index_in_dim(rows[:, 0], place, 0, keepdims=False)
        other = lax.dynamic_index_in_dim(rows[:, 0], place ^ 1, 0, keepdims=False)
        return swap_columns(own, other, col)

    values = own_clip(inputs).astype(jnp.float32)
    live_flag = lax.dynamic_index_in_dim(live_clips[:, 0], place, 0, keepdims=False)
    grad_final = own_clip(cotangent).astype(jnp.float32) * live_flag.astype(jnp.float32)
    first, kept_first = clip_forward(values, blocks[0], params[0])
    sent = first.astype(jnp.bfloat16)
    second, kept_second = clip_forward(sent.astype(jnp.float32), blocks[1], params[1])
    final = second.astype(jnp.bfloat16)
    states = in_order(
        trade([sent[:half], sent[half:], final[:half], final[half:]], place, (0, 1, 2, 3)), place
    )

    def reduce_grads(early, late):
        quarter = hidden_width // 2
        first_half = [
            jnp.concatenate([part[0], part[1], up_part[0][:, :quarter]], axis=1)
            for part, up_part in zip(late, early)
        ]
        second_half = [
            jnp.concatenate([up_part[0][:, quarter:], up_part[1]], axis=1) for up_part in early
        ]
        stacked = jnp.concatenate(first_half + second_half, axis=0)
        return lax.psum_scatter(stacked, EVERY, scatter_dimension=0, tiled=True)

    grad_mid, early, late, whole_second, split_second = clip_backward(
        grad_final, kept_second, blocks[1], params[1]
    )
    mid_low = grad_mid.astype(jnp.bfloat16)
    own_second = reduce_grads(early, late)
    mid_taken = trade([mid_low[:half], mid_low[half:]] * 2, place, (2, 3))
    grad_start, early, late, whole_first, split_first = clip_backward(
        mid_low.astype(jnp.float32), kept_first, blocks[0], params[0]
    )
    own_first = reduce_grads(early, late)
    start_low = grad_start.astype(jnp.bfloat16)
    start_taken = trade([start_low[:half], start_low[half:]] * 2, place, (0, 1))
    grads_in = in_order(
        [jnp.where(section == 1, mid, start) for mid, start in zip(mid_taken, start_taken)], place
    ).astype(jnp.float32)
    kept_half = jnp.where(section == 0, own_first, own_second)
    moved = lax.ppermute(
        jnp.where(section == 0, own_second, own_first), "pipe", [(0, 1), (1, 0)]
    )
    packed = jnp.where(
        section == 0,
        jnp.concatenate([kept_half, moved], axis=1),
        jnp.concatenate([moved, kept_half], axis=1),
    ).astype(jnp.float32)
    grad_qkv, grad_proj, grad_up, grad_down = cut_block(packed, width, hidden_width)
    whole_all, split_all = lax.psum(
        (jnp.stack([whole_first, whole_second]), jnp.stack([split_first, split_second])), EVERY
    )
    whole_out = lax.dynamic_index_in_dim(whole_all, section, 0, keepdims=False).reshape(
        6, 1, features
    )
    split_out = lax.dynamic_index_in_dim(split_all, section, 0, keepdims=False)
    split_out = lax.dynamic_index_in_dim(split_out, col, 0, keepdims=False)
    return (
        states[None, :, None],
        grads_in[None, :, None],
        whole_out[0],
        whole_out[1],
        jnp.stack([grad_qkv[:, part * width : (part + 1) * width] for part in range(3)])[None],
        split_out[None, :width],
        split_out[None, width : 2 * width],
        grad_proj.T[None],
        whole_out[2],
        whole_out[3],
        whole_out[4],
        grad_up[None],
        split_out[None, 2 * width :],
        grad_down.T[None],
        whole_out[5],
    )


def one_clip_each(mesh):
    sizes = dict(mesh.shape)
    return sizes["pipe"] == 2 and sizes["col"] == 2


def choose(mesh):
    def body(*arrays):
        fits = one_clip_each(mesh) and arrays[0].shape[:2] == (4, 1)
        return (on_device_clip if fits else on_device)(*arrays)

    return body


def solution(mesh):
    placed = (
        P(None, "row", "col", None),
        P("pipe", None),
        P("pipe", None),
        P("pipe", None, "row", "col"),
        P("pipe", "col"),
        P("pipe", "col"),
        P("pipe", "col", "row"),
        P("pipe", None),
        P("pipe", None),
        P("pipe", None),
        P("pipe", "row", "col"),
        P("pipe", "col"),
        P("pipe", "col", "row"),
        P("pipe", None),
        P(None, "row", "col", None),
        P(None, "row"),
    )
    return jax.shard_map(
        choose(mesh),
        mesh=mesh,
        in_specs=placed,
        out_specs=(
            P("pipe", None, "row", "col", None),
            P("pipe", None, "row", "col", None),
            P("pipe", None),
            P("pipe", None),
            P("pipe", None, "row", "col"),
            P("pipe", "col"),
            P("pipe", "col"),
            P("pipe", "col", "row"),
            P("pipe", None),
            P("pipe", None),
            P("pipe", None),
            P("pipe", "row", "col"),
            P("pipe", "col"),
            P("pipe", "col", "row"),
            P("pipe", None),
        ),
        check_vma=False,
    )
```
